32 devices in a mesh: gx: 4 (over z), gy: 4 (over x, core), sa: 2 (over y).
Axes of the slice: x: 2, y: 2, z: 4, core: 2. Of those that a mesh axis runs over, the one named last changes fastest.
Arguments:
- right_side: float32 [64, 256, 256], P('gx', 'gy', 'sa'), may hold values from -8 to 8
- diagonal: float32 [64, 256, 256], P('gx', 'gy', 'sa'), may hold values from 0.25 to 2
Outputs:
- pressure: float32 [64, 256, 256], P('gx', 'gy', 'sa')
- residual: float32 [64, 256, 256], P('gx', 'gy', 'sa')
The draws below stay inside these ranges and needn't reach their ends.
All inputs are finite; a program needn't handle non-finite values.
Results may differ from the reference program's by a relative error of at most 0.0001.
Values sent between devices are 32-bit elements; how exact they have to be, the bound alone decides.
A program may use at most 192 MiB of HBM per device.

```python
import jax
import jax.numpy as jnp

CYCLES = 2
SWEEPS = 5
COARSE_SWEEPS = 6
NX = 64
NY = 256
NZ = 256


def level_of(key, extent, cuts, least, top_value):
    def one(dim, parts):
        heights = jax.random.uniform(jax.random.fold_in(jax.random.fold_in(key, 6), dim), (parts,), jnp.float32, least / len(cuts), top_value / len(cuts))
        return jnp.repeat(jnp.exp(heights), extent[dim] // parts).reshape((-1,) + (1,) * (len(extent) - dim - 1))

    level = one(*cuts[0])
    for cut in cuts[1:]:
        level = level * one(*cut)
    return level


def normal_values(rng, shape, deviation, bound, cuts=(), kind=jnp.bfloat16):
    loudness = level_of(rng, shape, cuts, -0.22, 0.18) if cuts else 1.0
    values = jax.random.normal(rng, shape, jnp.float32) * deviation * loudness
    return jnp.minimum(jnp.maximum(values, -bound), bound).astype(kind)


def setup_inputs(seed: int = 0) -> dict:
    streams_of = jax.random.split(jax.random.key(seed), 3)
    right_side = normal_values(streams_of[0], (NX, NY, NZ), 1.0, 8.0, ((0, 4), (1, 4), (2, 2)), jnp.float32)
    diagonal = jnp.clip(0.25 + 1.75 * jax.random.uniform(streams_of[1], (NX, NY, NZ), jnp.float32) ** level_of(streams_of[1], (NX, NY, NZ), ((0, 4), (1, 4), (2, 2)), -0.2, 0.2), 0.25, 2.0)
    return dict(right_side=right_side, diagonal=diagonal)


damping = 2.0 / 3.0


def beside_sum(padded):
    total = padded[2:, 1:-1, 1:-1] + padded[:-2, 1:-1, 1:-1]
    total = total + padded[1:-1, 2:, 1:-1] + padded[1:-1, :-2, 1:-1]
    total = total + padded[1:-1, 1:-1, 2:] + padded[1:-1, 1:-1, :-2]
    return total


def operate(field, diag_field):
    return (6.0 + diag_field) * field - beside_sum(jnp.pad(field, 1))


def restrict(field):
    sx, sy, sz = field.shape
    return field.reshape(sx // 2, 2, sy // 2, 2, sz // 2, 2).sum(axis=(1, 3, 5)) * 0.5


def prolong(field):
    sx, sy, sz = field.shape
    wide = jnp.broadcast_to(field[:, None, :, None, :, None], (sx, 2, sy, 2, sz, 2))
    return wide.reshape(2 * sx, 2 * sy, 2 * sz)


def smooth(source, diag_field, count):
    correction = damping * source / (6.0 + diag_field)
    for sweep in range(count - 1):
        correction = correction + damping * (source - operate(correction, diag_field)) / (6.0 + diag_field)
    return correction


def reference(right_side, diagonal):
    coarse_diagonal = restrict(diagonal)
    pressure = jnp.zeros_like(right_side)
    rest = right_side
    for cycle in range(CYCLES):
        if cycle > 0:
            rest = right_side - operate(pressure, diagonal)
        fine_part = smooth(rest, diagonal, SWEEPS)
        coarse_part = smooth(restrict(rest), coarse_diagonal, COARSE_SWEEPS)
        pressure = pressure + fine_part + prolong(coarse_part)
    residual = right_side - operate(pressure, diagonal)
    return pressure, residual
```

```python
import functools

import jax
import jax.numpy as jnp
from jax import lax
from jax.experimental import pallas as pl
from jax.experimental.pallas import tpu as pltpu
from jax.sharding import PartitionSpec as P

CYCLES = 2
SWEEPS = 5
COARSE_SWEEPS = 6
STAGES = 3
W = 2.0 / 3.0
AXES = ("gx", "gy", "sa")
MESH = pl.DeviceIdType.MESH
S = 8
L = 128
COPIES = 32
F32 = jnp.float32
assert SWEEPS == 5 and COARSE_SWEEPS == 6


class Level:
    def __init__(self, at, nx, nj, dz, y0, refs):
        self.at, self.nx, self.nj, self.dz, self.y0 = at, nx, nj, dz, y0
        self.E, self.F, self.G, self.YC, self.ZC = refs


def level_scratch(nx, nj):
    return [
        pltpu.VMEM((3, nx + 4, nj, S, L), F32),
        pltpu.VMEM((CYCLES, nx + 2, nj, S, L), F32),
        pltpu.VMEM((nx + 2, nj, S, L), F32),
        pltpu.VMEM((2, nx, L), F32),
        pltpu.VMEM((S, L), F32),
    ]


def shared_scratch(rows):
    return [
        pltpu.VMEM((2, 2, 2, rows, L), F32),
        pltpu.VMEM((2, 2, 2, rows, L), F32),
        pltpu.VMEM((2, 4, S, L), F32),
        pltpu.VMEM((2, 4, S, L), F32),
        pltpu.VMEM((2, 2, 2, S, L), F32),
        pltpu.VMEM((2, 2, 2, S, L), F32),
        pltpu.VMEM((2, 2, 2, S, L), F32),
        pltpu.VMEM((2, 2, 2, S, L), F32),
        pltpu.VMEM((2, 2, rows, L), F32),
        pltpu.VMEM((CYCLES + 1, 2, rows, L), F32),
        pltpu.VMEM((CYCLES + 1, 2, rows, L), F32),
        pltpu.VMEM((CYCLES + 1, 2, S, L), F32),
        pltpu.VMEM((CYCLES + 1, 2, S, L), F32),
        pltpu.VMEM((2, 2, 2, S, L), F32),
    ]


def kernel(sizes, nx, nj, f_hbm, d_hbm, p_ref, r_ref, *scratch):
    fine = Level(0, nx, nj, 1, 0, scratch[0:5])
    coarse = Level(1, nx // 2, nj // 2, 2, nx, scratch[5:10])
    levels = (coarse, fine)
    YS, YR, ZS, ZR, CS, CR, ZXR, ZYR, YZR, FYS, FYR, FZS, FZR, ZXS = scratch[10:24]
    PB, PX, PY, PZ, YX, f_ref, d_ref, isem, ssem, rsem = scratch[24:]
    loads = [
        pltpu.make_async_copy(f_hbm, f_ref, isem.at[0]),
        pltpu.make_async_copy(d_hbm, d_ref, isem.at[1]),
    ]
    for load in loads:
        load.start()
    gx, gy, sa = (lax.axis_index(a) for a in AXES)
    ngx, ngy, _ = sizes
    left = sa == 0

    lane = lax.broadcasted_iota(jnp.int32, (S, L), 1)
    row = lax.broadcasted_iota(jnp.int32, (S, L), 0)
    even = lane & 1 == 0
    zero = jnp.zeros((S, L), F32)

    def present(d):
        dx, dy, _ = d
        tests = []
        if dx:
            tests.append(gx > 0 if dx < 0 else gx < ngx - 1)
        if dy:
            tests.append(gy > 0 if dy < 0 else gy < ngy - 1)
        if not tests:
            return None
        return functools.reduce(jnp.logical_and, tests)

    def device(d):
        return (gx + d[0], gy + d[1], 1 - sa if d[2] else sa)

    def when(cond, fn):
        if cond is None:
            fn()
        else:
            pl.when(cond)(fn)

    near = [(x, y, z) for x in (-1, 0, 1) for y in (-1, 0, 1) for z in (0, 1) if abs(x) + abs(y) + z in (1, 2)]

    def entries(rnd):
        cycle, stage = divmod(rnd, STAGES)
        q = rnd % 2
        out = []
        for u, dx in enumerate((-1, 1)):
            out.append(("edges", ZXS.at[q, u], ZXR.at[q, 1 - u], (dx, 0, 1)))
            for v, dy in enumerate((-1, 1)):
                out.append(("edges", CS.at[q, u, v], CR.at[q, 1 - u, 1 - v], (dx, dy, 0)))
        for lv in levels:
            n = lv.nx
            k = 1 if lv is fine and stage == STAGES - 1 else 2
            low, high = (2, k), (2 + n - k, k)
            to_low, to_high = (2 - k, k), (2 + n, k)
            if stage == 0:
                for ref in [lv.F.at[cycle]] + [lv.G] * (cycle == 0):
                    out.append(("planes", ref.at[1], ref.at[1 + n], (-1, 0, 0)))
                    out.append(("planes", ref.at[n], ref.at[0], (1, 0, 0)))
                low, high, to_low, to_high = (3, 1), (n, 1), (0, 1), (3 + n, 1)
            out.append(("planes", lv.E.at[q, pl.ds(*low)], lv.E.at[q, pl.ds(*to_high)], (-1, 0, 0)))
            out.append(("planes", lv.E.at[q, pl.ds(*high)], lv.E.at[q, pl.ds(*to_low)], (1, 0, 0)))
        out.append(("small", ZS.at[q], ZR.at[q], (0, 0, 1)))
        for v, dy in enumerate((-1, 1)):
            out.append(("small", YS.at[q, v, 0], YZR.at[q, 1 - v], (0, dy, 1)))
            out.append(("small", ZS.at[q, pl.ds(0, 2)], ZYR.at[q, 1 - v], (0, dy, 1)))
            out.append(("small", YS.at[q, v], YR.at[q, 1 - v], (0, dy, 0)))
        if stage == 0:
            for i in [cycle] + [CYCLES] * (cycle == 0):
                out.append(("small", FZS.at[i], FZR.at[i], (0, 0, 1)))
                for v, dy in enumerate((-1, 1)):
                    out.append(("small", FYS.at[i, v], FYR.at[i, 1 - v], (0, dy, 0)))
        assert len(out) <= COPIES
        return list(enumerate(out))

    def copy_of(rnd, i, entry):
        _, src, dst, d = entry
        return pltpu.make_async_remote_copy(
            src_ref=src,
            dst_ref=dst,
            send_sem=ssem.at[rnd, i],
            recv_sem=rsem.at[rnd, i],
            device_id=device(d),
            device_id_type=MESH,
        )

    def each(rnd, kinds, fn, sign=1):
        groups = {}
        for i, e in entries(rnd):
            if e[0] in kinds:
                groups.setdefault(e[3], []).append((i, e))
        for (dx, dy, dz), group in groups.items():

            def some(group=group):
                for i, e in group:
                    fn(copy_of(rnd, i, e))

            when(present((sign * dx, sign * dy, dz)), some)

    def send(rnd, *kinds):
        each(rnd, kinds, lambda c: c.start())

    def wait(rnd, *kinds):
        each(rnd, kinds, lambda c: c.wait_recv(), -1)

    def drain(rnd):
        each(rnd, ("edges", "planes", "small"), lambda c: c.wait_send())

    def turn(t, by):
        by %= L
        return t if by == 0 else pltpu.roll(t, by, 1)

    def from_edge(lv, depth):
        base = jnp.where(left, L - lv.dz * (depth + 1), lv.dz * depth)
        at = (lane - base) & (L - 1)
        return at if lv.dz == 1 else at >> 1

    edge = {lv: [from_edge(lv, depth) for depth in range(2)] for lv in levels}

    def pack(lv, k, t, accs):
        t = turn(t, lv.dz * k)
        return [jnp.where(edge[lv][i] == k, t, a) for i, a in enumerate(accs)]

    def packed(lv, acc, depth=0):
        return jnp.where(left, turn(acc, lv.dz * (depth + 1)), turn(acc, -lv.dz * depth))

    def put(lv, slot, q, x, tiles, accs):
        for j, t in enumerate(tiles):
            lv.E[slot, x + 2, j] = t
            accs = pack(lv, x * lv.nj + j, t, accs)
        at = slice(lv.y0 + x, lv.y0 + x + 1)
        for depth in range(2):
            YS[q, 0, depth, at, :] = tiles[depth][0:1]
            YS[q, 1, depth, at, :] = tiles[-1 - depth][S - 1 : S]
        if x in (0, lv.nx - 1):
            u = 0 if x == 0 else 1
            for v, t in enumerate((tiles[0][0:1], tiles[-1][S - 1 : S])):
                CS[q, u, v, lv.at : lv.at + 1, :] = t
            acc = zero
            for j, t in enumerate(tiles):
                (acc,) = pack(lv, j, t, [acc])
            ZXS[q, u, lv.at] = packed(lv, acc)
        return accs

    def put_end(lv, q, accs):
        for depth, acc in enumerate(accs):
            ZS[q, 2 * depth + lv.at] = packed(lv, acc, depth)

    def put_face(lv, i, x, tiles, acc):
        for j, t in enumerate(tiles):
            (acc,) = pack(lv, x * lv.nj + j, t, [acc])
        at = slice(lv.y0 + x, lv.y0 + x + 1)
        FYS[i, 0, at, :] = tiles[0][0:1]
        FYS[i, 1, at, :] = tiles[-1][S - 1 : S]
        return acc

    def outer(lv):
        return [0, 1, lv.nx - 2, lv.nx - 1]

    def inner(lv):
        return list(range(2, lv.nx - 2))

    def halo_of(lv, z):
        return jnp.where(left, turn(z, -lv.dz), z)

    def around(lv, slot, x, k, halo, rows):
        nj, dz = lv.nj, lv.dz
        mine = edge[lv][0] == 0
        c = [lv.E[slot, x + 2, j] for j in range(nj)]
        below = jnp.where(row == 0, rows[0], pltpu.roll(c[-1], 1, 0))
        above = jnp.where(row == S - 1, rows[1], pltpu.roll(c[0], S - 1, 0))
        ext = [below] + c + [above]
        sums = []
        for j in range(nj):
            t = lv.E[slot, x + 1, j] + lv.E[slot, x + 3, j] + (ext[j] + ext[j + 2])
            zl = jnp.where(lane < dz, 0.0, pltpu.roll(c[j], dz, 1))
            zr = jnp.where(lane >= L - dz, 0.0, pltpu.roll(c[j], L - dz, 1))
            h = turn(halo, -dz * (k + j))
            sums.append(t + (zl + zr) + jnp.where(mine, h, 0.0))
        return c, sums

    def step(lv, cycle, x, c, sums):
        return [
            (1.0 - W) * c[j] + lv.G[x + 1, j] * (lv.F[cycle, x + 1, j] + sums[j]) for j in range(lv.nj)
        ]

    def y_rows(lv, ref, x):
        at = lv.y0 + x
        return [ref[v, at : at + 1, :] for v in range(2)]

    def own_plane(lv, cycle, src, x, halo, rows):
        c, sums = around(lv, src, x, x * lv.nj, halo, rows)
        return step(lv, cycle, x, c, sums)

    def store(lv, slot, x, tiles):
        for j, t in enumerate(tiles):
            lv.E[slot, x + 2, j] = t

    def first_sweep(lv, cycle, q, xs):
        halo = halo_of(lv, ZR[q, lv.at])
        for x in xs:
            at = lv.y0 + x
            rows = [YR[q, v, 0, at : at + 1, :] for v in range(2)]
            store(lv, 2, x, own_plane(lv, cycle, q, x, halo, rows))

    def x_faces(lv, cycle, q):
        for u, x in enumerate((-1, lv.nx)):
            halo = halo_of(lv, ZXR[q, u, lv.at])
            rows = [CR[q, u, v, lv.at : lv.at + 1, :] for v in range(2)]
            c, sums = around(lv, q, x, 0, halo, rows)
            store(lv, 2, x, step(lv, cycle, x, c, sums))

    def y_faces(lv, cycle, q):
        tiles = lv.nx // S
        for v in range(2):
            at = [pl.ds(lv.y0 + S * t, S) for t in range(tiles)]
            c = [YR[q, v, 0, a, :] for a in at]
            for t, a in enumerate(at):
                before = CR[q, 0, v, lv.at : lv.at + 1, :] if t == 0 else pltpu.roll(c[t - 1], 1, 0)
                after = CR[q, 1, v, lv.at : lv.at + 1, :] if t == tiles - 1 else pltpu.roll(c[t + 1], S - 1, 0)
                xm = jnp.where(row == 0, before, pltpu.roll(c[t], 1, 0))
                xp = jnp.where(row == S - 1, after, pltpu.roll(c[t], S - 1, 0))
                z = YZR[q, v, a, :]
                zp = turn(jnp.where(lane < lv.dz, jnp.where(left, z, 0.0), c[t]), -lv.dz)
                zm = turn(jnp.where(lane >= L - lv.dz, jnp.where(left, 0.0, z), c[t]), lv.dz)
                sums = (xm + xp) + (YR[q, v, 1, a, :] + YS[q, v, 0, a, :]) + (zm + zp)
                g, f = FYR[CYCLES, v, a, :], FYR[cycle, v, a, :]
                lv.YC[v, pl.ds(S * t, S), :] = (1.0 - W) * c[t] + g * (f + sums)

    def z_face(lv, cycle, q):
        dz, n = lv.dz, lv.nj * lv.dz
        last = (lv.nx - 1) * n
        c = ZR[q, lv.at]
        xm = jnp.where(lane < n, ZXR[q, 0, lv.at], turn(c, n))
        xp = jnp.where(lane >= last, turn(ZXR[q, 1, lv.at], last), turn(c, -n))
        a = lane & (n - 1)
        low = turn(jnp.where(row == S - 1, ZYR[q, 0, lv.at], c), dz - n)
        high = turn(jnp.where(row == 0, ZYR[q, 1, lv.at], c), n - dz)
        ym = jnp.where(a < dz, pltpu.roll(low, 1, 0), turn(c, dz))
        yp = jnp.where(a >= n - dz, pltpu.roll(high, S - 1, 0), turn(c, -dz))
        sums = (xm + xp) + (ym + yp) + (ZR[q, 2 + lv.at] + ZS[q, lv.at])
        lv.ZC[...] = (1.0 - W) * c + FZR[CYCLES, lv.at] * (FZR[cycle, lv.at] + sums)

    def second_sweep(lv, cycle, q, xs, accs):
        halo = halo_of(lv, lv.ZC[...])
        for x in xs:
            rows = [lv.YC[v, x : x + 1, :] for v in range(2)]
            accs = put(lv, q, q, x, own_plane(lv, cycle, 2, x, halo, rows), accs)
        return accs

    def restrict(tiles):
        t = (tiles[0] + tiles[1]) + (tiles[2] + tiles[3])
        return 0.5 * (t + jnp.where(even, pltpu.roll(t, L - 1, 1), pltpu.roll(t, 1, 1)))

    def begin_coarse(cycle, q, xs, carry):
        first = cycle == 0
        accs, fz, gz = carry
        for X in xs:
            new, fs, gs = [], [], []
            for J in range(nj // 2):
                cells = [(2 * X + i, 2 * J + k) for i in range(2) for k in range(2)]
                if first:
                    at = [(x, pl.ds(j, S, stride=nj)) for x, j in cells]
                    cf = restrict([f_ref[x, y, :] for x, y in at])
                    cd = restrict([d_ref[x, y, :] for x, y in at])
                    g = W / (6.0 + cd)
                    coarse.G[X + 1, J] = g
                else:
                    cf = restrict([fine.F[cycle, x + 1, j] for x, j in cells])
                    g = coarse.G[X + 1, J]
                coarse.F[cycle, X + 1, J] = cf
                fs.append(cf)
                gs.append(g)
                new.append(g * cf)
            accs = put(coarse, q, q, X, new, accs)
            fz = put_face(coarse, cycle, X, fs, fz)
            if first:
                gz = put_face(coarse, CYCLES, X, gs, gz)
        return accs, fz, gz

    def begin_fine(cycle, q, xs, carry):
        first = cycle == 0
        accs, fz, gz = carry
        for x in xs:
            new, fs, gs = [], [], []
            for j in range(nj):
                if first:
                    y = pl.ds(j, S, stride=nj)
                    f = f_ref[x, y, :]
                    g = W / (6.0 + d_ref[x, y, :])
                    fine.F[cycle, x + 1, j] = f
                    fine.G[x + 1, j] = g
                else:
                    f = fine.F[cycle, x + 1, j]
                    g = fine.G[x + 1, j]
                fs.append(f)
                gs.append(g)
                new.append(g * f)
            accs = put(fine, q, q, x, new, accs)
            fz = put_face(fine, cycle, x, fs, fz)
            if first:
                gz = put_face(fine, CYCLES, x, gs, gz)
        return accs, fz, gz

    def begin(cycle, before=None):
        rnd = STAGES * cycle
        q = rnd % 2
        start = ([zero] * 2, zero, zero)
        if before is not None:
            before([0, 1, 2, 3, nx - 4, nx - 3, nx - 2, nx - 1])
        low = begin_coarse(cycle, q, outer(coarse), start)
        high = begin_fine(cycle, q, outer(fine), start)
        if cycle == 0:
            pl.semaphore_wait(barrier, count)
        send(rnd, "edges", "planes")
        if before is not None:
            before(range(4, nx - 4))
        low = begin_coarse(cycle, q, inner(coarse), low)
        high = begin_fine(cycle, q, inner(fine), high)
        for lv, (accs, fz, gz) in ((coarse, low), (fine, high)):
            put_end(lv, q, accs)
            FZS[cycle, lv.at] = packed(lv, fz)
            if cycle == 0:
                FZS[CYCLES, lv.at] = packed(lv, gz)
        send(rnd, "small")

    for lv in levels:
        for slot in range(2):
            for plane in (0, 1, lv.nx + 2, lv.nx + 3):
                lv.E[slot, plane] = jnp.zeros((lv.nj, S, L), F32)
        for plane in (0, lv.nx + 1):
            for cycle in range(CYCLES):
                lv.F[cycle, plane] = jnp.zeros((lv.nj, S, L), F32)
            lv.G[plane] = jnp.zeros((lv.nj, S, L), F32)
    for ref in (YR, CR, CS, ZXR, ZYR, YZR, FYR):
        ref[...] = jnp.zeros(ref.shape, F32)

    barrier = pltpu.get_barrier_semaphore()
    count = 0
    for d in near:
        cond = present(d)
        when(cond, lambda d=d: pl.semaphore_signal(barrier, inc=1, device_id=device(d), device_id_type=MESH))
        count = count + (1 if cond is None else cond.astype(jnp.int32))
    for load in loads:
        load.wait()

    begin(0)
    for cycle in range(CYCLES):
        for stage in range(STAGES):
            rnd = STAGES * cycle + stage
            q = rnd % 2
            last = stage == STAGES - 1
            swept = levels[: 1 if last else 2]
            wait(rnd, "edges", "small")
            for lv in swept:
                first_sweep(lv, cycle, q, range(1, lv.nx - 1))
                y_faces(lv, cycle, q)
                z_face(lv, cycle, q)
            wait(rnd, "planes")
            if stage == 0:
                for lv in levels:
                    for x in (-1, lv.nx):
                        for j in range(lv.nj):
                            lv.E[q, x + 2, j] = lv.G[x + 1, j] * lv.F[cycle, x + 1, j]
            for lv in swept:
                first_sweep(lv, cycle, q, (0, lv.nx - 1))
                x_faces(lv, cycle, q)
            if not last:
                accs = [second_sweep(lv, cycle, 1 - q, outer(lv), [zero] * 2) for lv in levels]
                send(rnd + 1, "edges", "planes")
                for lv, acc in zip(levels, accs):
                    put_end(lv, 1 - q, second_sweep(lv, cycle, 1 - q, inner(lv), acc))
                send(rnd + 1, "small")
                drain(rnd)

        for x in range(-1, nx + 1):
            own = 0 <= x < nx
            for j in range(nj):
                t = fine.E[q, x + 2, j] + coarse.E[2, x // 2 + 2, j // 2]
                if cycle > 0:
                    t = t + (PB[x, j] if own else PX[0 if x < 0 else 1, j])
                fine.E[2, x + 2, j] = t
                if not own:
                    PX[0 if x < 0 else 1, j] = t
                elif cycle < CYCLES - 1:
                    PB[x, j] = t
                else:
                    p_ref[x, pl.ds(j, S, stride=nj), :] = t
        for v in range(2):
            for i in range(2):
                YX[v, pl.ds(i, coarse.nx, stride=2), :] = coarse.YC[v]
            t = YR[q, v, 0, 0:nx, :] + YX[v]
            PY[v] = t if cycle == 0 else t + PY[v]
        z = coarse.ZC[...]
        t = zero
        for x in range(nx):
            here = (lane >= nj * x) & (lane < nj * (x + 1))
            t = jnp.where(here, turn(z, nj * (x - x // 2)), t)
        t = t + ZR[q, 0]
        PZ[...] = t if cycle == 0 else t + PZ[...]

        def rest(xs, cycle=cycle):
            halo = halo_of(fine, PZ[...])
            for x in xs:
                c, sums = around(fine, 2, x, x * nj, halo, [PY[v, x : x + 1, :] for v in range(2)])
                for j in range(nj):
                    at = pl.ds(j, S, stride=nj)
                    r = f_ref[x, at, :] - ((6.0 + d_ref[x, at, :]) * c[j] - sums[j])
                    if cycle < CYCLES - 1:
                        fine.F[cycle + 1, x + 1, j] = r
                    else:
                        r_ref[x, at, :] = r

        if cycle < CYCLES - 1:
            begin(cycle + 1, rest)
        else:
            rest(range(nx))
        drain(STAGES * cycle + STAGES - 1)


def solution(mesh):
    sizes = tuple(mesh.shape[a] for a in AXES)
    assert sizes[2] == 2

    def body(right_side, diagonal):
        nx, ny, nz = right_side.shape
        nj = ny // S
        assert nz == L and ny % (2 * S) == 0 and nx % (2 * S) == 0 and nx * nj == L and nj & (nj - 1) == 0
        shape = jax.ShapeDtypeStruct(right_side.shape, F32)
        vmem = pl.BlockSpec(memory_space=pltpu.VMEM)
        hbm = pl.BlockSpec(memory_space=pltpu.HBM)
        return pl.pallas_call(
            functools.partial(kernel, sizes, nx, nj),
            out_shape=(shape, shape),
            in_specs=[hbm, hbm],
            out_specs=(vmem, vmem),
            scratch_shapes=level_scratch(nx, nj)
            + level_scratch(nx // 2, nj // 2)
            + shared_scratch(nx + nx // 2)
            + [
                pltpu.VMEM((nx, nj, S, L), F32),
                pltpu.VMEM((2, nj, S, L), F32),
                pltpu.VMEM((2, nx, L), F32),
                pltpu.VMEM((S, L), F32),
                pltpu.VMEM((2, nx, L), F32),
                pltpu.VMEM(right_side.shape, F32),
                pltpu.VMEM(right_side.shape, F32),
                pltpu.SemaphoreType.DMA((2,)),
                pltpu.SemaphoreType.DMA((CYCLES * STAGES, COPIES)),
                pltpu.SemaphoreType.DMA((CYCLES * STAGES, COPIES)),
            ],
            compiler_params=pltpu.CompilerParams(
                collective_id=0, has_side_effects=True, vmem_limit_bytes=32 * 1024 * 1024
            ),
        )(right_side, diagonal)

    return jax.shard_map(
        body,
        mesh=mesh,
        in_specs=(P(*AXES), P(*AXES)),
        out_specs=(P(*AXES), P(*AXES)),
        check_vma=False,
    )
```

```python
import functools

import jax
import jax.numpy as jnp
from jax import lax
from jax.experimental import pallas as pl
from jax.experimental.pallas import tpu as pltpu
from jax.sharding import PartitionSpec as P

CYCLES = 2
SWEEPS = 5
COARSE_SWEEPS = 6
STAGES = 3
W = 2.0 / 3.0
AXES = ("gx", "gy", "sa")
MESH = pl.DeviceIdType.MESH
S = 8
L = 128
COPIES = 22
F32 = jnp.float32
assert SWEEPS == 5 and COARSE_SWEEPS == 6


def field_of(cycle):
    return CYCLES - 1 - cycle


class Level:
    def __init__(self, at, nx, nj, dz, y0, refs):
        self.at, self.nx, self.nj, self.dz, self.y0 = at, nx, nj, dz, y0
        self.E, self.FG, self.YC, self.ZC, self.ZN = refs
        self.F = [self.FG.at[field_of(cycle)] for cycle in range(CYCLES)]
        self.G = self.FG.at[CYCLES]


def level_scratch(nx, nj):
    return [
        pltpu.VMEM((3, nx + 4, nj, S, L), F32),
        pltpu.VMEM((CYCLES + 1, nx + 2, nj, S, L), F32),
        pltpu.VMEM((2, nx, L), F32),
        pltpu.VMEM((S, L), F32),
        pltpu.VMEM((S, L), F32),
    ]


def shared_scratch(rows, halves):
    return [
        pltpu.VMEM((2, 2, 2, rows, L), F32),
        pltpu.VMEM((2, 2, 2, rows, L), F32),
        pltpu.VMEM((2, 4, S, L), F32),
        pltpu.VMEM((2, 4, S, L), F32),
        pltpu.VMEM((2, 2, 2, S, L), F32),
        pltpu.VMEM((2, 2, 2, S, L), F32),
        pltpu.VMEM((2, 2, 2, S, L), F32),
        pltpu.VMEM((2, 2, 2, S, L), F32),
        pltpu.VMEM((2, 2, rows, L), F32),
        pltpu.VMEM((CYCLES + 1, 2, rows, L), F32),
        pltpu.VMEM((CYCLES + 1, 2, rows, L), F32),
        pltpu.VMEM((CYCLES + 1, 2, S, L), F32),
        pltpu.VMEM((CYCLES + 1, 2, S, L), F32),
        pltpu.VMEM((2, 2, 2, S, L), F32),
        pltpu.VMEM((2, 2, 3, halves, S, L), F32),
        pltpu.VMEM((2, 2, 3, halves, S, L), F32),
    ]


def kernel(sizes, nx, nj, f_hbm, d_hbm, p_ref, r_ref, *scratch):
    fine = Level(0, nx, nj, 1, 0, scratch[0:5])
    coarse = Level(1, nx // 2, nj // 2, 2, nx, scratch[5:10])
    levels = (coarse, fine)
    YS, YR, ZS, ZR, CS, CR, ZXR, ZYR, YZR, FYS, FYR, FZS, FZR, ZXS, XS, XR = scratch[10:26]
    PB, PX, PY, PZ, YX, f_ref, d_ref, isem, ssem, rsem = scratch[26:]
    loads = [
        pltpu.make_async_copy(f_hbm, f_ref, isem.at[0]),
        pltpu.make_async_copy(d_hbm, d_ref, isem.at[1]),
    ]
    for load in loads:
        load.start()
    gx, gy, sa = (lax.axis_index(a) for a in AXES)
    ngx, ngy, _ = sizes
    left = sa == 0

    lane = lax.broadcasted_iota(jnp.int32, (S, L), 1)
    row = lax.broadcasted_iota(jnp.int32, (S, L), 0)
    even = lane & 1 == 0
    zero = jnp.zeros((S, L), F32)

    def present(d):
        dx, dy, _ = d
        tests = []
        if dx:
            tests.append(gx > 0 if dx < 0 else gx < ngx - 1)
        if dy:
            tests.append(gy > 0 if dy < 0 else gy < ngy - 1)
        if not tests:
            return None
        return functools.reduce(jnp.logical_and, tests)

    def device(d):
        return (gx + d[0], gy + d[1], 1 - sa if d[2] else sa)

    def when(cond, fn):
        if cond is None:
            fn()
        else:
            pl.when(cond)(fn)

    near = [(x, y, z) for x in (-1, 0, 1) for y in (-1, 0, 1) for z in (0, 1) if abs(x) + abs(y) + z in (1, 2)]

    def entries(rnd):
        cycle, stage = divmod(rnd, STAGES)
        q = rnd % 2
        out = []
        for u, dx in enumerate((-1, 1)):
            out.append(("edges", ZXS.at[q, u], ZXR.at[q, 1 - u], (dx, 0, 1)))
            for v, dy in enumerate((-1, 1)):
                out.append(("edges", CS.at[q, u, v], CR.at[q, 1 - u, 1 - v], (dx, dy, 0)))
        fields = pl.ds(field_of(cycle), 2 if cycle == 0 else 1)
        count = 2 if stage or cycle else 3
        for u, dx in enumerate((-1, 1)):
            out.append(("planes", XS.at[q, u, pl.ds(0, count)], XR.at[q, 1 - u, pl.ds(0, count)], (dx, 0, 0)))
        k = 1 if stage == STAGES - 1 else 2
        low, high = (2, k), (2 + nx - k, k)
        to_low, to_high = (2 - k, k), (2 + nx, k)
        if stage == 0:
            out.append(("planes", fine.FG.at[fields, 1], fine.FG.at[fields, 1 + nx], (-1, 0, 0)))
            out.append(("planes", fine.FG.at[fields, nx], fine.FG.at[fields, 0], (1, 0, 0)))
            low, high, to_low, to_high = (3, 1), (nx, 1), (0, 1), (3 + nx, 1)
        out.append(("planes", fine.E.at[q, pl.ds(*low)], fine.E.at[q, pl.ds(*to_high)], (-1, 0, 0)))
        out.append(("planes", fine.E.at[q, pl.ds(*high)], fine.E.at[q, pl.ds(*to_low)], (1, 0, 0)))
        out.append(("small", ZS.at[q], ZR.at[q], (0, 0, 1)))
        for v, dy in enumerate((-1, 1)):
            out.append(("small", YS.at[q, v, 0], YZR.at[q, 1 - v], (0, dy, 1)))
            out.append(("small", ZS.at[q, pl.ds(0, 2)], ZYR.at[q, 1 - v], (0, dy, 1)))
            out.append(("small", YS.at[q, v], YR.at[q, 1 - v], (0, dy, 0)))
        if stage == 0:
            out.append(("small", FZS.at[fields], FZR.at[fields], (0, 0, 1)))
            for v, dy in enumerate((-1, 1)):
                out.append(("small", FYS.at[fields, v], FYR.at[fields, 1 - v], (0, dy, 0)))
        assert len(out) <= COPIES
        return list(enumerate(out))

    def copy_of(rnd, i, entry):
        _, src, dst, d = entry
        return pltpu.make_async_remote_copy(
            src_ref=src,
            dst_ref=dst,
            send_sem=ssem.at[rnd % 2, i],
            recv_sem=rsem.at[rnd % 2, i],
            device_id=device(d),
            device_id_type=MESH,
        )

    def each(rnd, kinds, fn, sign=1):
        groups = {}
        for i, e in entries(rnd):
            if e[0] in kinds:
                groups.setdefault(e[3], []).append((i, e))
        for (dx, dy, dz), group in groups.items():

            def some(group=group):
                for i, e in group:
                    fn(copy_of(rnd, i, e))

            when(present((sign * dx, sign * dy, dz)), some)

    def send(rnd, *kinds):
        each(rnd, kinds, lambda c: c.start())

    def wait(rnd, *kinds):
        each(rnd, kinds, lambda c: c.wait_recv(), -1)

    def drain(rnd):
        each(rnd, ("edges", "planes", "small"), lambda c: c.wait_send())

    def turn(t, by):
        by %= L
        return t if by == 0 else pltpu.roll(t, by, 1)

    def from_edge(lv, depth):
        base = jnp.where(left, L - lv.dz * (depth + 1), lv.dz * depth)
        at = (lane - base) & (L - 1)
        return at if lv.dz == 1 else at >> 1

    edge = {lv: [from_edge(lv, depth) for depth in range(2)] for lv in levels}

    def pack(lv, k, t, accs):
        t = turn(t, lv.dz * k)
        return [jnp.where(edge[lv][i] == k, t, a) for i, a in enumerate(accs)]

    def packed(lv, acc, depth=0):
        return jnp.where(left, turn(acc, lv.dz * (depth + 1)), turn(acc, -lv.dz * depth))

    def squeeze(q, u, slot, tiles):
        for i in range(0, len(tiles), 2):
            XS[q, u, slot, i // 2] = jnp.where(even, tiles[i], tiles[i + 1])

    def widen(q, u, slot):
        out = []
        for i in range(coarse.nj // 2):
            t = XR[q, u, slot, i]
            out.append(jnp.where(even, t, pltpu.roll(t, 1, 1)))
            out.append(jnp.where(even, pltpu.roll(t, L - 1, 1), t))
        return out

    def put(lv, slot, q, x, tiles, accs, first=False):
        for j, t in enumerate(tiles):
            lv.E[slot, x + 2, j] = t
            accs = pack(lv, x * lv.nj + j, t, accs)
        at = slice(lv.y0 + x, lv.y0 + x + 1)
        for depth in range(2):
            YS[q, 0, depth, at, :] = tiles[depth][0:1]
            YS[q, 1, depth, at, :] = tiles[-1 - depth][S - 1 : S]
        if lv is coarse and (x < 2 or x >= lv.nx - 2):
            depth = x if x < 2 else lv.nx - 1 - x
            if not first:
                squeeze(q, 0 if x < 2 else 1, depth, tiles)
            elif depth == 1:
                squeeze(q, 0 if x < 2 else 1, 0, tiles)
        if x in (0, lv.nx - 1):
            u = 0 if x == 0 else 1
            for v, t in enumerate((tiles[0][0:1], tiles[-1][S - 1 : S])):
                CS[q, u, v, lv.at : lv.at + 1, :] = t
            acc = zero
            for j, t in enumerate(tiles):
                (acc,) = pack(lv, j, t, [acc])
            ZXS[q, u, lv.at] = packed(lv, acc)
        return accs

    def put_end(lv, q, accs):
        for depth, acc in enumerate(accs):
            ZS[q, 2 * depth + lv.at] = packed(lv, acc, depth)

    def put_face(lv, q, i, x, tiles, acc):
        for j, t in enumerate(tiles):
            (acc,) = pack(lv, x * lv.nj + j, t, [acc])
        at = slice(lv.y0 + x, lv.y0 + x + 1)
        FYS[i, 0, at, :] = tiles[0][0:1]
        FYS[i, 1, at, :] = tiles[-1][S - 1 : S]
        if lv is coarse and x in (0, lv.nx - 1):
            squeeze(q, 0 if x == 0 else 1, 2 if i == CYCLES else 1, tiles)
        return acc

    def outer(lv):
        return [0, 1, lv.nx - 2, lv.nx - 1]

    def inner(lv):
        return list(range(2, lv.nx - 2))

    def halo_of(lv, z):
        return jnp.where(left, turn(z, -lv.dz), z)

    def around(lv, slot, x, k, halo, rows):
        nj, dz = lv.nj, lv.dz
        mine = edge[lv][0] == 0
        c = [lv.E[slot, x + 2, j] for j in range(nj)]
        below = jnp.where(row == 0, rows[0], pltpu.roll(c[-1], 1, 0))
        above = jnp.where(row == S - 1, rows[1], pltpu.roll(c[0], S - 1, 0))
        ext = [below] + c + [above]
        sums = []
        for j in range(nj):
            t = lv.E[slot, x + 1, j] + lv.E[slot, x + 3, j] + (ext[j] + ext[j + 2])
            zl = jnp.where(lane < dz, 0.0, pltpu.roll(c[j], dz, 1))
            zr = jnp.where(lane >= L - dz, 0.0, pltpu.roll(c[j], L - dz, 1))
            h = turn(halo, -dz * (k + j))
            sums.append(t + (zl + zr) + jnp.where(mine, h, 0.0))
        return c, sums

    def step(lv, cycle, x, c, sums):
        return [
            (1.0 - W) * c[j] + lv.G[x + 1, j] * (lv.F[cycle][x + 1, j] + sums[j]) for j in range(lv.nj)
        ]

    def y_rows(lv, ref, x):
        at = lv.y0 + x
        return [ref[v, at : at + 1, :] for v in range(2)]

    def own_plane(lv, cycle, src, x, halo, rows):
        c, sums = around(lv, src, x, x * lv.nj, halo, rows)
        return step(lv, cycle, x, c, sums)

    def store(lv, slot, x, tiles):
        for j, t in enumerate(tiles):
            lv.E[slot, x + 2, j] = t

    def first_sweep(lv, cycle, q, xs):
        halo = halo_of(lv, ZR[q, lv.at])
        for x in xs:
            at = lv.y0 + x
            rows = [YR[q, v, 0, at : at + 1, :] for v in range(2)]
            store(lv, 2, x, own_plane(lv, cycle, q, x, halo, rows))

    def x_faces(lv, cycle, q):
        for u, x in enumerate((-1, lv.nx)):
            halo = halo_of(lv, ZXR[q, u, lv.at])
            rows = [CR[q, u, v, lv.at : lv.at + 1, :] for v in range(2)]
            c, sums = around(lv, q, x, 0, halo, rows)
            store(lv, 2, x, step(lv, cycle, x, c, sums))

    def y_faces(lv, cycle, q):
        tiles = lv.nx // S
        for v in range(2):
            at = [pl.ds(lv.y0 + S * t, S) for t in range(tiles)]
            c = [YR[q, v, 0, a, :] for a in at]
            for t, a in enumerate(at):
                before = CR[q, 0, v, lv.at : lv.at + 1, :] if t == 0 else pltpu.roll(c[t - 1], 1, 0)
                after = CR[q, 1, v, lv.at : lv.at + 1, :] if t == tiles - 1 else pltpu.roll(c[t + 1], S - 1, 0)
                xm = jnp.where(row == 0, before, pltpu.roll(c[t], 1, 0))
                xp = jnp.where(row == S - 1, after, pltpu.roll(c[t], S - 1, 0))
                z = YZR[q, v, a, :]
                zp = turn(jnp.where(lane < lv.dz, jnp.where(left, z, 0.0), c[t]), -lv.dz)
                zm = turn(jnp.where(lane >= L - lv.dz, jnp.where(left, 0.0, z), c[t]), lv.dz)
                sums = (xm + xp) + (YR[q, v, 1, a, :] + YS[q, v, 0, a, :]) + (zm + zp)
                g, f = FYR[CYCLES, v, a, :], FYR[field_of(cycle), v, a, :]
                lv.YC[v, pl.ds(S * t, S), :] = (1.0 - W) * c[t] + g * (f + sums)

    def z_face(lv, cycle, q):
        dz, n = lv.dz, lv.nj * lv.dz
        last = (lv.nx - 1) * n
        c = ZR[q, lv.at]
        xm = jnp.where(lane < n, ZXR[q, 0, lv.at], turn(c, n))
        xp = jnp.where(lane >= last, turn(ZXR[q, 1, lv.at], last), turn(c, -n))
        a = lane & (n - 1)
        low = turn(jnp.where(row == S - 1, ZYR[q, 0, lv.at], c), dz - n)
        high = turn(jnp.where(row == 0, ZYR[q, 1, lv.at], c), n - dz)
        ym = jnp.where(a < dz, pltpu.roll(low, 1, 0), turn(c, dz))
        yp = jnp.where(a >= n - dz, pltpu.roll(high, S - 1, 0), turn(c, -dz))
        sums = (xm + xp) + (ym + yp) + (ZR[q, 2 + lv.at] + ZS[q, lv.at])
        new = (1.0 - W) * c + FZR[CYCLES, lv.at] * (FZR[field_of(cycle), lv.at] + sums)
        lv.ZC[...] = halo_of(lv, new)
        lv.ZN[...] = new

    def second_sweep(lv, cycle, q, xs, accs):
        halo = lv.ZC[...]
        for x in xs:
            rows = [lv.YC[v, x : x + 1, :] for v in range(2)]
            accs = put(lv, q, q, x, own_plane(lv, cycle, 2, x, halo, rows), accs)
        return accs

    def restrict(tiles):
        t = (tiles[0] + tiles[1]) + (tiles[2] + tiles[3])
        return 0.5 * (t + jnp.where(even, pltpu.roll(t, L - 1, 1), pltpu.roll(t, 1, 1)))

    def begin_coarse(cycle, q, xs, carry):
        first = cycle == 0
        accs, fz, gz = carry
        for X in xs:
            new, fs, gs = [], [], []
            for J in range(nj // 2):
                cells = [(2 * X + i, 2 * J + k) for i in range(2) for k in range(2)]
                if first:
                    at = [(x, pl.ds(j, S, stride=nj)) for x, j in cells]
                    cf = restrict([f_ref[x, y, :] for x, y in at])
                    cd = restrict([d_ref[x, y, :] for x, y in at])
                    g = W / (6.0 + cd)
                    coarse.G[X + 1, J] = g
                else:
                    cf = restrict([fine.F[cycle][x + 1, j] for x, j in cells])
                    g = coarse.G[X + 1, J]
                coarse.F[cycle][X + 1, J] = cf
                fs.append(cf)
                gs.append(g)
                new.append(g * cf)
            accs = put(coarse, q, q, X, new, accs, True)
            fz = put_face(coarse, q, field_of(cycle), X, fs, fz)
            if first:
                gz = put_face(coarse, q, CYCLES, X, gs, gz)
        return accs, fz, gz

    def begin_fine(cycle, q, xs, carry):
        first = cycle == 0
        accs, fz, gz = carry
        for x in xs:
            new, fs, gs = [], [], []
            for j in range(nj):
                if first:
                    y = pl.ds(j, S, stride=nj)
                    f = f_ref[x, y, :]
                    g = W / (6.0 + d_ref[x, y, :])
                    fine.F[cycle][x + 1, j] = f
                    fine.G[x + 1, j] = g
                else:
                    f = fine.F[cycle][x + 1, j]
                    g = fine.G[x + 1, j]
                fs.append(f)
                gs.append(g)
                new.append(g * f)
            accs = put(fine, q, q, x, new, accs, True)
            fz = put_face(fine, q, field_of(cycle), x, fs, fz)
            if first:
                gz = put_face(fine, q, CYCLES, x, gs, gz)
        return accs, fz, gz

    def begin(cycle, before=None):
        rnd = STAGES * cycle
        q = rnd % 2
        start = ([zero] * 2, zero, zero)
        if before is not None:
            before([0, 1, 2, 3, nx - 4, nx - 3, nx - 2, nx - 1])
        low = begin_coarse(cycle, q, outer(coarse), start)
        high = begin_fine(cycle, q, outer(fine), start)
        if cycle == 0:
            pl.semaphore_wait(barrier, count)
        send(rnd, "edges", "planes")
        if before is not None:
            before(range(4, nx - 4))
        low = begin_coarse(cycle, q, inner(coarse), low)
        high = begin_fine(cycle, q, inner(fine), high)
        for lv, (accs, fz, gz) in ((coarse, low), (fine, high)):
            put_end(lv, q, accs)
            FZS[field_of(cycle), lv.at] = packed(lv, fz)
            if cycle == 0:
                FZS[CYCLES, lv.at] = packed(lv, gz)
        send(rnd, "small")

    for lv in levels:
        for slot in range(2):
            for plane in (0, 1, lv.nx + 2, lv.nx + 3):
                lv.E[slot, plane] = jnp.zeros((lv.nj, S, L), F32)
        for plane in (0, lv.nx + 1):
            for cycle in range(CYCLES):
                lv.F[cycle][plane] = jnp.zeros((lv.nj, S, L), F32)
            lv.G[plane] = jnp.zeros((lv.nj, S, L), F32)
    for ref in (YR, CR, CS, ZXR, ZYR, YZR, FYR, XR):
        ref[...] = jnp.zeros(ref.shape, F32)

    barrier = pltpu.get_barrier_semaphore()
    count = 0
    for d in near:
        cond = present(d)
        when(cond, lambda d=d: pl.semaphore_signal(barrier, inc=1, device_id=device(d), device_id_type=MESH))
        count = count + (1 if cond is None else cond.astype(jnp.int32))
    for load in loads:
        load.wait()

    begin(0)
    for cycle in range(CYCLES):
        for stage in range(STAGES):
            rnd = STAGES * cycle + stage
            q = rnd % 2
            last = stage == STAGES - 1
            swept = levels[: 1 if last else 2]
            wait(rnd, "edges", "small")
            for lv in swept:
                z_face(lv, cycle, q)
            for lv in swept:
                y_faces(lv, cycle, q)
            for lv in swept:
                first_sweep(lv, cycle, q, range(1, lv.nx - 1))
            wait(rnd, "planes")
            for u in range(2):
                beside, beyond = (1, 0) if u == 0 else (coarse.nx + 2, coarse.nx + 3)
                for j, t in enumerate(widen(q, u, 0)):
                    coarse.E[q, beyond if stage == 0 else beside, j] = t
                for j, t in enumerate(widen(q, u, 1)):
                    if stage == 0:
                        coarse.F[cycle][u * (coarse.nx + 1), j] = t
                    else:
                        coarse.E[q, beyond, j] = t
                if stage == 0 and cycle == 0:
                    for j, t in enumerate(widen(q, u, 2)):
                        coarse.G[u * (coarse.nx + 1), j] = t
            if stage == 0:
                for lv in levels:
                    for x in (-1, lv.nx):
                        for j in range(lv.nj):
                            lv.E[q, x + 2, j] = lv.G[x + 1, j] * lv.F[cycle][x + 1, j]
            for lv in swept:
                x_faces(lv, cycle, q)
            for lv in swept:
                first_sweep(lv, cycle, q, (0, lv.nx - 1))
            if not last:
                accs = [second_sweep(lv, cycle, 1 - q, outer(lv), [zero] * 2) for lv in levels]
                send(rnd + 1, "edges", "planes")
                for lv, acc in zip(levels, accs):
                    put_end(lv, 1 - q, second_sweep(lv, cycle, 1 - q, inner(lv), acc))
                send(rnd + 1, "small")
                drain(rnd)

        for v in range(2):
            for i in range(2):
                YX[v, pl.ds(i, coarse.nx, stride=2), :] = coarse.YC[v]
            t = YR[q, v, 0, 0:nx, :] + YX[v]
            PY[v] = t if cycle == 0 else t + PY[v]
        z = coarse.ZN[...]
        t = zero
        for x in range(nx):
            here = (lane >= nj * x) & (lane < nj * (x + 1))
            t = jnp.where(here, turn(z, nj * (x - x // 2)), t)
        t = t + ZR[q, 0]
        t = t if cycle == 0 else t + PZ[0]
        PZ[0] = t
        PZ[1] = halo_of(fine, t)
        for x in range(-1, nx + 1):
            own = 0 <= x < nx
            for j in range(nj):
                t = fine.E[q, x + 2, j] + coarse.E[2, x // 2 + 2, j // 2]
                if cycle > 0:
                    t = t + (PB[x, j] if own else PX[0 if x < 0 else 1, j])
                fine.E[2, x + 2, j] = t
                if not own:
                    PX[0 if x < 0 else 1, j] = t
                elif cycle < CYCLES - 1:
                    PB[x, j] = t
                else:
                    p_ref[x, pl.ds(j, S, stride=nj), :] = t

        def rest(xs, cycle=cycle):
            halo = PZ[1]
            for x in xs:
                c, sums = around(fine, 2, x, x * nj, halo, [PY[v, x : x + 1, :] for v in range(2)])
                for j in range(nj):
                    at = pl.ds(j, S, stride=nj)
                    r = f_ref[x, at, :] - ((6.0 + d_ref[x, at, :]) * c[j] - sums[j])
                    if cycle < CYCLES - 1:
                        fine.F[cycle + 1][x + 1, j] = r
                    else:
                        r_ref[x, at, :] = r

        if cycle < CYCLES - 1:
            begin(cycle + 1, rest)
        else:
            rest(range(nx))
        drain(STAGES * cycle + STAGES - 1)


def solution(mesh):
    sizes = tuple(mesh.shape[a] for a in AXES)
    assert sizes[2] == 2

    def body(right_side, diagonal):
        nx, ny, nz = right_side.shape
        nj = ny // S
        assert nz == L and ny % (2 * S) == 0 and nx % (2 * S) == 0 and nx * nj == L and nj & (nj - 1) == 0 and nj >= 4
        shape = jax.ShapeDtypeStruct(right_side.shape, F32)
        vmem = pl.BlockSpec(memory_space=pltpu.VMEM)
        hbm = pl.BlockSpec(memory_space=pltpu.HBM)
        return pl.pallas_call(
            functools.partial(kernel, sizes, nx, nj),
            out_shape=(shape, shape),
            in_specs=[hbm, hbm],
            out_specs=(vmem, vmem),
            scratch_shapes=level_scratch(nx, nj)
            + level_scratch(nx // 2, nj // 2)
            + shared_scratch(nx + nx // 2, nj // 4)
            + [
                pltpu.VMEM((nx, nj, S, L), F32),
                pltpu.VMEM((2, nj, S, L), F32),
                pltpu.VMEM((2, nx, L), F32),
                pltpu.VMEM((2, S, L), F32),
                pltpu.VMEM((2, nx, L), F32),
                pltpu.VMEM(right_side.shape, F32),
                pltpu.VMEM(right_side.shape, F32),
                pltpu.SemaphoreType.DMA((2,)),
                pltpu.SemaphoreType.DMA((2, COPIES)),
                pltpu.SemaphoreType.DMA((2, COPIES)),
            ],
            compiler_params=pltpu.CompilerParams(
                collective_id=0, has_side_effects=True, vmem_limit_bytes=32 * 1024 * 1024
            ),
        )(right_side, diagonal)

    return jax.shard_map(
        body,
        mesh=mesh,
        in_specs=(P(*AXES), P(*AXES)),
        out_specs=(P(*AXES), P(*AXES)),
        check_vma=False,
    )
```

```python
import functools

import jax
import jax.numpy as jnp
from jax import lax
from jax.experimental import pallas as pl
from jax.experimental.pallas import tpu as pltpu
from jax.sharding import PartitionSpec as P

CYCLES = 2
SWEEPS = 5
COARSE_SWEEPS = 6
STAGES = 3
W = 2.0 / 3.0
AXES = ("gx", "gy", "sa")
MESH = pl.DeviceIdType.MESH
S = 8
L = 128
COPIES = 22
F32 = jnp.float32
assert SWEEPS == 5 and COARSE_SWEEPS == 6


def field_of(cycle):
    return CYCLES - 1 - cycle


class Level:
    def __init__(self, at, nx, nj, dz, y0, refs):
        self.at, self.nx, self.nj, self.dz, self.y0 = at, nx, nj, dz, y0
        self.E, self.FG, self.YC, self.ZC, self.ZN = refs
        self.F = [self.FG.at[field_of(cycle)] for cycle in range(CYCLES)]
        self.G = self.FG.at[CYCLES]


def level_scratch(nx, nj):
    return [
        pltpu.VMEM((3, nx + 4, nj, S, L), F32),
        pltpu.VMEM((CYCLES + 1, nx + 2, nj, S, L), F32),
        pltpu.VMEM((2, nx, L), F32),
        pltpu.VMEM((S, L), F32),
        pltpu.VMEM((S, L), F32),
    ]


def shared_scratch(rows, halves):
    return [
        pltpu.VMEM((2, 2, 2, rows, L), F32),
        pltpu.VMEM((2, 2, 2, rows, L), F32),
        pltpu.VMEM((2, 4, S, L), F32),
        pltpu.VMEM((2, 4, S, L), F32),
        pltpu.VMEM((2, 2, 2, S, L), F32),
        pltpu.VMEM((2, 2, 2, S, L), F32),
        pltpu.VMEM((2, 2, 2, S, L), F32),
        pltpu.VMEM((2, 2, 2, S, L), F32),
        pltpu.VMEM((2, 2, rows, L), F32),
        pltpu.VMEM((CYCLES + 1, 2, rows, L), F32),
        pltpu.VMEM((CYCLES + 1, 2, rows, L), F32),
        pltpu.VMEM((CYCLES + 1, 2, S, L), F32),
        pltpu.VMEM((CYCLES + 1, 2, S, L), F32),
        pltpu.VMEM((2, 2, 2, S, L), F32),
        pltpu.VMEM((2, 2, 3, halves, S, L), F32),
        pltpu.VMEM((2, 2, 3, halves, S, L), F32),
    ]


def kernel(sizes, nx, nj, f_hbm, d_hbm, p_ref, r_ref, *scratch):
    fine = Level(0, nx, nj, 1, 0, scratch[0:5])
    coarse = Level(1, nx // 2, nj // 2, 2, nx, scratch[5:10])
    levels = (coarse, fine)
    YS, YR, ZS, ZR, CS, CR, ZXR, ZYR, YZR, FYS, FYR, FZS, FZR, ZXS, XS, XR = scratch[10:26]
    PB, PX, PY, PZ, YX, f_ref, d_ref, isem, ssem, rsem = scratch[26:]
    loads = [
        pltpu.make_async_copy(f_hbm, f_ref, isem.at[0]),
        pltpu.make_async_copy(d_hbm, d_ref, isem.at[1]),
    ]
    for load in loads:
        load.start()
    gx, gy, sa = (lax.axis_index(a) for a in AXES)
    ngx, ngy, _ = sizes
    left = sa == 0

    lane = lax.broadcasted_iota(jnp.int32, (S, L), 1)
    row = lax.broadcasted_iota(jnp.int32, (S, L), 0)
    even = lane & 1 == 0
    zero = jnp.zeros((S, L), F32)

    def present(d):
        dx, dy, _ = d
        tests = []
        if dx:
            tests.append(gx > 0 if dx < 0 else gx < ngx - 1)
        if dy:
            tests.append(gy > 0 if dy < 0 else gy < ngy - 1)
        if not tests:
            return None
        return functools.reduce(jnp.logical_and, tests)

    def device(d):
        return (gx + d[0], gy + d[1], 1 - sa if d[2] else sa)

    def when(cond, fn):
        if cond is None:
            fn()
        else:
            pl.when(cond)(fn)

    near = [(x, y, z) for x in (-1, 0, 1) for y in (-1, 0, 1) for z in (0, 1) if abs(x) + abs(y) + z in (1, 2)]

    def entries(rnd):
        cycle, stage = divmod(rnd, STAGES)
        q = rnd % 2
        out = []
        for u, dx in enumerate((-1, 1)):
            out.append(("edges", ZXS.at[q, u], ZXR.at[q, 1 - u], (dx, 0, 1)))
            for v, dy in enumerate((-1, 1)):
                out.append(("edges", CS.at[q, u, v], CR.at[q, 1 - u, 1 - v], (dx, dy, 0)))
        fields = pl.ds(field_of(cycle), 2 if cycle == 0 else 1)
        count = 2 if stage or cycle else 3
        for u, dx in enumerate((-1, 1)):
            out.append(("planes", XS.at[q, u, pl.ds(0, count)], XR.at[q, 1 - u, pl.ds(0, count)], (dx, 0, 0)))
        if stage == 0:
            out.append(("planes", fine.FG.at[fields, 1], fine.FG.at[fields, 1 + nx], (-1, 0, 0)))
            out.append(("planes", fine.FG.at[fields, nx], fine.FG.at[fields, 0], (1, 0, 0)))
        for depth in range(2):
            if (stage, depth) in ((0, 0), (STAGES - 1, 1)):
                continue
            kind = "beyond" if depth else "planes"
            out.append((kind, fine.E.at[q, 2 + depth], fine.E.at[q, 2 + nx + depth], (-1, 0, 0)))
            out.append((kind, fine.E.at[q, 1 + nx - depth], fine.E.at[q, 1 - depth], (1, 0, 0)))
        out.append(("small", ZS.at[q], ZR.at[q], (0, 0, 1)))
        for v, dy in enumerate((-1, 1)):
            out.append(("small", YS.at[q, v, 0], YZR.at[q, 1 - v], (0, dy, 1)))
            out.append(("small", ZS.at[q, pl.ds(0, 2)], ZYR.at[q, 1 - v], (0, dy, 1)))
            out.append(("small", YS.at[q, v], YR.at[q, 1 - v], (0, dy, 0)))
        if stage == 0:
            out.append(("small", FZS.at[fields], FZR.at[fields], (0, 0, 1)))
            for v, dy in enumerate((-1, 1)):
                out.append(("small", FYS.at[fields, v], FYR.at[fields, 1 - v], (0, dy, 0)))
        assert len(out) <= COPIES
        return list(enumerate(out))

    def copy_of(rnd, i, entry):
        _, src, dst, d = entry
        return pltpu.make_async_remote_copy(
            src_ref=src,
            dst_ref=dst,
            send_sem=ssem.at[rnd % 2, i],
            recv_sem=rsem.at[rnd % 2, i],
            device_id=device(d),
            device_id_type=MESH,
        )

    def each(rnd, kinds, fn, sign=1):
        groups = {}
        for i, e in entries(rnd):
            if e[0] in kinds:
                groups.setdefault(e[3], []).append((i, e))
        for (dx, dy, dz), group in groups.items():

            def some(group=group):
                for i, e in group:
                    fn(copy_of(rnd, i, e))

            when(present((sign * dx, sign * dy, dz)), some)

    def send(rnd, *kinds):
        each(rnd, kinds, lambda c: c.start())

    def wait(rnd, *kinds):
        each(rnd, kinds, lambda c: c.wait_recv(), -1)

    def drain(rnd):
        each(rnd, ("edges", "planes", "small", "beyond"), lambda c: c.wait_send())

    def turn(t, by):
        by %= L
        return t if by == 0 else pltpu.roll(t, by, 1)

    def from_edge(lv, depth):
        base = jnp.where(left, L - lv.dz * (depth + 1), lv.dz * depth)
        at = (lane - base) & (L - 1)
        return at if lv.dz == 1 else at >> 1

    edge = {lv: [from_edge(lv, depth) for depth in range(2)] for lv in levels}

    def pack(lv, k, t, accs):
        t = turn(t, lv.dz * k)
        return [jnp.where(edge[lv][i] == k, t, a) for i, a in enumerate(accs)]

    def packed(lv, acc, depth=0):
        return jnp.where(left, turn(acc, lv.dz * (depth + 1)), turn(acc, -lv.dz * depth))

    def squeeze(q, u, slot, tiles):
        for i in range(0, len(tiles), 2):
            XS[q, u, slot, i // 2] = jnp.where(even, tiles[i], tiles[i + 1])

    def widen(q, u, slot):
        out = []
        for i in range(coarse.nj // 2):
            t = XR[q, u, slot, i]
            out.append(jnp.where(even, t, pltpu.roll(t, 1, 1)))
            out.append(jnp.where(even, pltpu.roll(t, L - 1, 1), t))
        return out

    def put(lv, slot, q, x, tiles, accs, first=False):
        for j, t in enumerate(tiles):
            lv.E[slot, x + 2, j] = t
            accs = pack(lv, x * lv.nj + j, t, accs)
        at = slice(lv.y0 + x, lv.y0 + x + 1)
        for depth in range(2):
            YS[q, 0, depth, at, :] = tiles[depth][0:1]
            YS[q, 1, depth, at, :] = tiles[-1 - depth][S - 1 : S]
        if lv is coarse and (x < 2 or x >= lv.nx - 2):
            depth = x if x < 2 else lv.nx - 1 - x
            if not first:
                squeeze(q, 0 if x < 2 else 1, depth, tiles)
            elif depth == 1:
                squeeze(q, 0 if x < 2 else 1, 0, tiles)
        if x in (0, lv.nx - 1):
            u = 0 if x == 0 else 1
            for v, t in enumerate((tiles[0][0:1], tiles[-1][S - 1 : S])):
                CS[q, u, v, lv.at : lv.at + 1, :] = t
            acc = zero
            for j, t in enumerate(tiles):
                (acc,) = pack(lv, j, t, [acc])
            ZXS[q, u, lv.at] = packed(lv, acc)
        return accs

    def put_end(lv, q, accs):
        for depth, acc in enumerate(accs):
            ZS[q, 2 * depth + lv.at] = packed(lv, acc, depth)

    def put_face(lv, q, i, x, tiles, acc):
        for j, t in enumerate(tiles):
            (acc,) = pack(lv, x * lv.nj + j, t, [acc])
        at = slice(lv.y0 + x, lv.y0 + x + 1)
        FYS[i, 0, at, :] = tiles[0][0:1]
        FYS[i, 1, at, :] = tiles[-1][S - 1 : S]
        if lv is coarse and x in (0, lv.nx - 1):
            squeeze(q, 0 if x == 0 else 1, 2 if i == CYCLES else 1, tiles)
        return acc

    def outer(lv):
        n = lv.nx
        return [0, n - 1] if lv is fine else [0, 1, n - 2, n - 1]

    def inner(lv):
        return [x for x in (1, lv.nx - 2, *range(2, lv.nx - 2)) if x not in outer(lv)]

    def halo_of(lv, z):
        return jnp.where(left, turn(z, -lv.dz), z)

    def around(lv, slot, x, k, halo, rows):
        nj, dz = lv.nj, lv.dz
        mine = edge[lv][0] == 0
        c = [lv.E[slot, x + 2, j] for j in range(nj)]
        below = jnp.where(row == 0, rows[0], pltpu.roll(c[-1], 1, 0))
        above = jnp.where(row == S - 1, rows[1], pltpu.roll(c[0], S - 1, 0))
        ext = [below] + c + [above]
        sums = []
        for j in range(nj):
            t = lv.E[slot, x + 1, j] + lv.E[slot, x + 3, j] + (ext[j] + ext[j + 2])
            zl = jnp.where(lane < dz, 0.0, pltpu.roll(c[j], dz, 1))
            zr = jnp.where(lane >= L - dz, 0.0, pltpu.roll(c[j], L - dz, 1))
            h = turn(halo, -dz * (k + j))
            sums.append(t + (zl + zr) + jnp.where(mine, h, 0.0))
        return c, sums

    def step(lv, cycle, x, c, sums):
        return [
            (1.0 - W) * c[j] + lv.G[x + 1, j] * (lv.F[cycle][x + 1, j] + sums[j]) for j in range(lv.nj)
        ]

    def y_rows(lv, ref, x):
        at = lv.y0 + x
        return [ref[v, at : at + 1, :] for v in range(2)]

    def own_plane(lv, cycle, src, x, halo, rows):
        c, sums = around(lv, src, x, x * lv.nj, halo, rows)
        return step(lv, cycle, x, c, sums)

    def store(lv, slot, x, tiles):
        for j, t in enumerate(tiles):
            lv.E[slot, x + 2, j] = t

    def first_sweep(lv, cycle, q, xs):
        halo = halo_of(lv, ZR[q, lv.at])
        for x in xs:
            at = lv.y0 + x
            rows = [YR[q, v, 0, at : at + 1, :] for v in range(2)]
            store(lv, 2, x, own_plane(lv, cycle, q, x, halo, rows))

    def x_faces(lv, cycle, q):
        for u, x in enumerate((-1, lv.nx)):
            halo = halo_of(lv, ZXR[q, u, lv.at])
            rows = [CR[q, u, v, lv.at : lv.at + 1, :] for v in range(2)]
            c, sums = around(lv, q, x, 0, halo, rows)
            store(lv, 2, x, step(lv, cycle, x, c, sums))

    def y_faces(lv, cycle, q):
        tiles = lv.nx // S
        for v in range(2):
            at = [pl.ds(lv.y0 + S * t, S) for t in range(tiles)]
            c = [YR[q, v, 0, a, :] for a in at]
            for t, a in enumerate(at):
                before = CR[q, 0, v, lv.at : lv.at + 1, :] if t == 0 else pltpu.roll(c[t - 1], 1, 0)
                after = CR[q, 1, v, lv.at : lv.at + 1, :] if t == tiles - 1 else pltpu.roll(c[t + 1], S - 1, 0)
                xm = jnp.where(row == 0, before, pltpu.roll(c[t], 1, 0))
                xp = jnp.where(row == S - 1, after, pltpu.roll(c[t], S - 1, 0))
                z = YZR[q, v, a, :]
                zp = turn(jnp.where(lane < lv.dz, jnp.where(left, z, 0.0), c[t]), -lv.dz)
                zm = turn(jnp.where(lane >= L - lv.dz, jnp.where(left, 0.0, z), c[t]), lv.dz)
                sums = (xm + xp) + (YR[q, v, 1, a, :] + YS[q, v, 0, a, :]) + (zm + zp)
                g, f = FYR[CYCLES, v, a, :], FYR[field_of(cycle), v, a, :]
                lv.YC[v, pl.ds(S * t, S), :] = (1.0 - W) * c[t] + g * (f + sums)

    def z_face(lv, cycle, q):
        dz, n = lv.dz, lv.nj * lv.dz
        last = (lv.nx - 1) * n
        c = ZR[q, lv.at]
        xm = jnp.where(lane < n, ZXR[q, 0, lv.at], turn(c, n))
        xp = jnp.where(lane >= last, turn(ZXR[q, 1, lv.at], last), turn(c, -n))
        a = lane & (n - 1)
        low = turn(jnp.where(row == S - 1, ZYR[q, 0, lv.at], c), dz - n)
        high = turn(jnp.where(row == 0, ZYR[q, 1, lv.at], c), n - dz)
        ym = jnp.where(a < dz, pltpu.roll(low, 1, 0), turn(c, dz))
        yp = jnp.where(a >= n - dz, pltpu.roll(high, S - 1, 0), turn(c, -dz))
        sums = (xm + xp) + (ym + yp) + (ZR[q, 2 + lv.at] + ZS[q, lv.at])
        new = (1.0 - W) * c + FZR[CYCLES, lv.at] * (FZR[field_of(cycle), lv.at] + sums)
        lv.ZC[...] = halo_of(lv, new)
        lv.ZN[...] = new

    def second_sweep(lv, cycle, q, xs, accs):
        halo = lv.ZC[...]
        for x in xs:
            rows = [lv.YC[v, x : x + 1, :] for v in range(2)]
            accs = put(lv, q, q, x, own_plane(lv, cycle, 2, x, halo, rows), accs)
        return accs

    def restrict(tiles):
        t = (tiles[0] + tiles[1]) + (tiles[2] + tiles[3])
        return 0.5 * (t + jnp.where(even, pltpu.roll(t, L - 1, 1), pltpu.roll(t, 1, 1)))

    def begin_coarse(cycle, q, xs, carry):
        first = cycle == 0
        accs, fz, gz = carry
        for X in xs:
            new, fs, gs = [], [], []
            for J in range(nj // 2):
                cells = [(2 * X + i, 2 * J + k) for i in range(2) for k in range(2)]
                if first:
                    at = [(x, pl.ds(j, S, stride=nj)) for x, j in cells]
                    cf = restrict([f_ref[x, y, :] for x, y in at])
                    cd = restrict([d_ref[x, y, :] for x, y in at])
                    g = W / (6.0 + cd)
                    coarse.G[X + 1, J] = g
                else:
                    cf = restrict([fine.F[cycle][x + 1, j] for x, j in cells])
                    g = coarse.G[X + 1, J]
                coarse.F[cycle][X + 1, J] = cf
                fs.append(cf)
                gs.append(g)
                new.append(g * cf)
            accs = put(coarse, q, q, X, new, accs, True)
            fz = put_face(coarse, q, field_of(cycle), X, fs, fz)
            if first:
                gz = put_face(coarse, q, CYCLES, X, gs, gz)
        return accs, fz, gz

    def begin_fine(cycle, q, xs, carry):
        first = cycle == 0
        accs, fz, gz = carry
        for x in xs:
            new, fs, gs = [], [], []
            for j in range(nj):
                if first:
                    y = pl.ds(j, S, stride=nj)
                    f = f_ref[x, y, :]
                    g = W / (6.0 + d_ref[x, y, :])
                    fine.F[cycle][x + 1, j] = f
                    fine.G[x + 1, j] = g
                else:
                    f = fine.F[cycle][x + 1, j]
                    g = fine.G[x + 1, j]
                fs.append(f)
                gs.append(g)
                new.append(g * f)
            accs = put(fine, q, q, x, new, accs, True)
            fz = put_face(fine, q, field_of(cycle), x, fs, fz)
            if first:
                gz = put_face(fine, q, CYCLES, x, gs, gz)
        return accs, fz, gz

    def begin(cycle, before=None):
        rnd = STAGES * cycle
        q = rnd % 2
        start = ([zero] * 2, zero, zero)
        if before is not None:
            before([0, 1, 2, 3, nx - 4, nx - 3, nx - 2, nx - 1])
        low = begin_coarse(cycle, q, outer(coarse), start)
        high = begin_fine(cycle, q, outer(fine), start)
        if cycle == 0:
            pl.semaphore_wait(barrier, count)
        send(rnd, "edges", "planes")
        if before is not None:
            before(range(4, nx - 4))
        low = begin_coarse(cycle, q, inner(coarse), low)
        high = begin_fine(cycle, q, inner(fine), high)
        for lv, (accs, fz, gz) in ((coarse, low), (fine, high)):
            put_end(lv, q, accs)
            FZS[field_of(cycle), lv.at] = packed(lv, fz)
            if cycle == 0:
                FZS[CYCLES, lv.at] = packed(lv, gz)
        send(rnd, "small")
        send(rnd, "beyond")

    for lv in levels:
        for slot in range(2):
            for plane in (0, 1, lv.nx + 2, lv.nx + 3):
                lv.E[slot, plane] = jnp.zeros((lv.nj, S, L), F32)
        for plane in (0, lv.nx + 1):
            for cycle in range(CYCLES):
                lv.F[cycle][plane] = jnp.zeros((lv.nj, S, L), F32)
            lv.G[plane] = jnp.zeros((lv.nj, S, L), F32)
    for ref in (YR, CR, CS, ZXR, ZYR, YZR, FYR, XR):
        ref[...] = jnp.zeros(ref.shape, F32)

    barrier = pltpu.get_barrier_semaphore()
    count = 0
    for d in near:
        cond = present(d)
        when(cond, lambda d=d: pl.semaphore_signal(barrier, inc=1, device_id=device(d), device_id_type=MESH))
        count = count + (1 if cond is None else cond.astype(jnp.int32))
    for load in loads:
        load.wait()

    begin(0)
    for cycle in range(CYCLES):
        for stage in range(STAGES):
            rnd = STAGES * cycle + stage
            q = rnd % 2
            last = stage == STAGES - 1
            swept = levels[: 1 if last else 2]
            wait(rnd, "edges", "small")
            for lv in swept:
                z_face(lv, cycle, q)
            for lv in swept:
                y_faces(lv, cycle, q)
            for lv in swept:
                first_sweep(lv, cycle, q, range(1, lv.nx - 1))
            wait(rnd, "planes", "beyond")
            for u in range(2):
                beside, beyond = (1, 0) if u == 0 else (coarse.nx + 2, coarse.nx + 3)
                for j, t in enumerate(widen(q, u, 0)):
                    coarse.E[q, beyond if stage == 0 else beside, j] = t
                for j, t in enumerate(widen(q, u, 1)):
                    if stage == 0:
                        coarse.F[cycle][u * (coarse.nx + 1), j] = t
                    else:
                        coarse.E[q, beyond, j] = t
                if stage == 0 and cycle == 0:
                    for j, t in enumerate(widen(q, u, 2)):
                        coarse.G[u * (coarse.nx + 1), j] = t
            if stage == 0:
                for lv in levels:
                    for x in (-1, lv.nx):
                        for j in range(lv.nj):
                            lv.E[q, x + 2, j] = lv.G[x + 1, j] * lv.F[cycle][x + 1, j]
            for lv in swept:
                x_faces(lv, cycle, q)
            for lv in swept:
                first_sweep(lv, cycle, q, (0, lv.nx - 1))
            if not last:
                accs = [second_sweep(lv, cycle, 1 - q, outer(lv), [zero] * 2) for lv in levels]
                send(rnd + 1, "edges", "planes")
                for lv, acc in zip(levels, accs):
                    put_end(lv, 1 - q, second_sweep(lv, cycle, 1 - q, inner(lv), acc))
                send(rnd + 1, "small")
                send(rnd + 1, "beyond")
                drain(rnd)

        for v in range(2):
            for i in range(2):
                YX[v, pl.ds(i, coarse.nx, stride=2), :] = coarse.YC[v]
            t = YR[q, v, 0, 0:nx, :] + YX[v]
            PY[v] = t if cycle == 0 else t + PY[v]
        z = coarse.ZN[...]
        t = zero
        for x in range(nx):
            here = (lane >= nj * x) & (lane < nj * (x + 1))
            t = jnp.where(here, turn(z, nj * (x - x // 2)), t)
        t = t + ZR[q, 0]
        t = t if cycle == 0 else t + PZ[0]
        PZ[0] = t
        PZ[1] = halo_of(fine, t)
        for x in range(-1, nx + 1):
            own = 0 <= x < nx
            for j in range(nj):
                t = fine.E[q, x + 2, j] + coarse.E[2, x // 2 + 2, j // 2]
                if cycle > 0:
                    t = t + (PB[x, j] if own else PX[0 if x < 0 else 1, j])
                fine.E[2, x + 2, j] = t
                if not own:
                    PX[0 if x < 0 else 1, j] = t
                elif cycle < CYCLES - 1:
                    PB[x, j] = t
                else:
                    p_ref[x, pl.ds(j, S, stride=nj), :] = t

        def rest(xs, cycle=cycle):
            halo = PZ[1]
            for x in xs:
                c, sums = around(fine, 2, x, x * nj, halo, [PY[v, x : x + 1, :] for v in range(2)])
                for j in range(nj):
                    at = pl.ds(j, S, stride=nj)
                    r = f_ref[x, at, :] - ((6.0 + d_ref[x, at, :]) * c[j] - sums[j])
                    if cycle < CYCLES - 1:
                        fine.F[cycle + 1][x + 1, j] = r
                    else:
                        r_ref[x, at, :] = r

        if cycle < CYCLES - 1:
            begin(cycle + 1, rest)
        else:
            rest(range(nx))
        drain(STAGES * cycle + STAGES - 1)


def solution(mesh):
    sizes = tuple(mesh.shape[a] for a in AXES)
    assert sizes[2] == 2

    def body(right_side, diagonal):
        nx, ny, nz = right_side.shape
        nj = ny // S
        assert nz == L and ny % (2 * S) == 0 and nx % (2 * S) == 0 and nx * nj == L and nj & (nj - 1) == 0 and nj >= 4
        shape = jax.ShapeDtypeStruct(right_side.shape, F32)
        vmem = pl.BlockSpec(memory_space=pltpu.VMEM)
        hbm = pl.BlockSpec(memory_space=pltpu.HBM)
        return pl.pallas_call(
            functools.partial(kernel, sizes, nx, nj),
            out_shape=(shape, shape),
            in_specs=[hbm, hbm],
            out_specs=(vmem, vmem),
            scratch_shapes=level_scratch(nx, nj)
            + level_scratch(nx // 2, nj // 2)
            + shared_scratch(nx + nx // 2, nj // 4)
            + [
                pltpu.VMEM((nx, nj, S, L), F32),
                pltpu.VMEM((2, nj, S, L), F32),
                pltpu.VMEM((2, nx, L), F32),
                pltpu.VMEM((2, S, L), F32),
                pltpu.VMEM((2, nx, L), F32),
                pltpu.VMEM(right_side.shape, F32),
                pltpu.VMEM(right_side.shape, F32),
                pltpu.SemaphoreType.DMA((2,)),
                pltpu.SemaphoreType.DMA((2, COPIES)),
                pltpu.SemaphoreType.DMA((2, COPIES)),
            ],
            compiler_params=pltpu.CompilerParams(
                collective_id=0, has_side_effects=True, vmem_limit_bytes=32 * 1024 * 1024
            ),
        )(right_side, diagonal)

    return jax.shard_map(
        body,
        mesh=mesh,
        in_specs=(P(*AXES), P(*AXES)),
        out_specs=(P(*AXES), P(*AXES)),
        check_vma=False,
    )
```
